32 devices in a mesh: groups: 2 (over y), mp: 4 (over z), example: 4 (over x, core).
Axes of the slice: x: 2, y: 2, z: 4, core: 2. Of those that a mesh axis runs over, the one named last changes fastest.
Arguments:
- inputs: bfloat16 [2, 24576, 28672], P(None, ('groups', 'example'), 'mp'), parts along dimension 1, may hold values from -6 to 6
- out_grads: bfloat16 [2, 24576, 8192], P(None, ('groups', 'example', 'mp')), parts along dimension 1, may hold values from -6 to 6
- lengths: int32 [24], P(('groups', 'example')), parts along dimension 0, may hold values from 128 to 1024, as said below
- proj_in: bfloat16 [2, 28672, 64], P(None, 'mp'), may hold values from -0.03125 to 0.03125
- proj_out: bfloat16 [2, 8192, 64], replicated, may hold values from -0.0625 to 0.0625
- queries: bfloat16 [1024, 8192], P('example', 'mp'), may hold values from -0.0029296875 to 0.0029296875
Outputs:
- logged: bfloat16 [24, 8192], P(('groups', 'example'), 'mp'), parts along dimension 0
- scores: float32 [24, 1024], P(('groups', 'example')), parts along dimension 0
The draws below stay inside these ranges and needn't reach their ends.
There are 2 independent parts, one for each index of `groups`. The reference program is written for one: setup_inputs(seed, part) draws one part's arguments, and reference() takes and returns one part's arrays. A program takes and returns all parts, laid end to end along the dimension named above; an argument that names none is the same for every part. Nothing has to cross between parts.
Inputs may be any that keep to these rules, and one draw needn't show every extreme that they name: `lengths`: slots at or past an example's length are padding; in every draw some example is full (1024).
All inputs are finite; a program needn't handle non-finite values.
Results may differ from the reference program's by a relative error of at most 0.005.
Values may be sent and summed in bfloat16 or wider, within the bound.
No kernel may reach another device: no remote copies, remote signals or barrier semaphores. Data moves between devices by JAX's collectives and lax.ppermute only.
A program may use at most 256 MiB of HBM per device.

```python
import jax
import jax.numpy as jnp
from jax import lax

D = 8192
FF = 28672
RANK = 64
L = 2
SEQ = 1024
QUERIES = 1024
EXAMPLES = 12
TOKENS = 12288
FEAT = 8192


def draw_lengths(key, part):
    first_key, second_key = jax.random.split(jax.random.fold_in(key, 17))
    values = jax.random.randint(first_key, (EXAMPLES,), SEQ // 8, SEQ + 1)
    picked = jax.random.randint(second_key, (), 0, EXAMPLES)
    return jnp.where(jnp.arange(EXAMPLES) == picked, SEQ, values).astype(jnp.int32)


def steps_of(key, extent, cuts, least, high):
    factor_of, own = 1.0, jax.random.fold_in(key, 6)
    for position, parts in cuts:
        heights = jnp.exp(jax.random.uniform(jax.random.fold_in(own, position), (parts,), jnp.float32, least / len(cuts), high / len(cuts)))
        factor_of = factor_of * jnp.repeat(heights, extent[position] // parts).reshape([-1 if axis == position else 1 for axis in range(len(extent))])
    return factor_of


def bell_draw(rng, extent, width, most, shards=(), held_as=jnp.bfloat16):
    values = width * jax.random.normal(rng, extent, jnp.float32)
    if shards:
        values = values * steps_of(rng, extent, shards, -0.22, 0.18)
    return jnp.clip(values, -most, most).astype(held_as)


def setup_inputs(seed: int = 0, part: int = 0) -> dict:
    splits = jax.random.split(jax.random.key(seed), 7)
    part_keys = jax.random.split(jax.random.fold_in(splits[6], part), 7)
    return {
        "inputs": bell_draw(part_keys[0], (L, TOKENS, FF), 1.0, 6.0, ((1, 4), (2, 4))),
        "out_grads": bell_draw(part_keys[1], (L, TOKENS, D), 1.0, 6.0, ((1, 16),)),
        "lengths": draw_lengths(jax.random.fold_in(jax.random.fold_in(splits[6], part), 71), part),
        "proj_in": bell_draw(splits[3], (L, FF, RANK), FF ** -0.5, 0.03125, ((1, 4),)),
        "proj_out": bell_draw(splits[4], (L, D, RANK), D ** -0.5, 0.0625),
        "queries": bell_draw(splits[5], (QUERIES, FEAT), (FEAT * SEQ // 2) ** -0.5, 0.0029296875, ((0, 4), (1, 4))),
    }


def reference(inputs, out_grads, lengths, proj_in, proj_out, queries):
    positions = jnp.arange(TOKENS, dtype=jnp.int32)
    is_live = (positions % SEQ) < lengths[positions // SEQ]

    def one_layer(operands):
        layer_in, layer_grad, weight_in, weight_out = operands
        input_side = jnp.dot(layer_in, weight_in, preferred_element_type=jnp.float32)
        output_side = jnp.dot(layer_grad, weight_out, preferred_element_type=jnp.float32)
        output_side = jnp.where(is_live[:, None], output_side, jnp.float32(0.0)).astype(jnp.bfloat16)
        output_side = lax.optimization_barrier(output_side).astype(jnp.float32)
        return jnp.einsum("esi,esj->eij", output_side.reshape(EXAMPLES, SEQ, RANK),
                          input_side.reshape(EXAMPLES, SEQ, RANK), precision=lax.Precision.HIGHEST)

    per_layer = lax.map(one_layer, (inputs, out_grads, proj_in, proj_out))
    logged = jnp.transpose(per_layer, (1, 0, 2, 3)).reshape(EXAMPLES, FEAT).astype(jnp.bfloat16)
    scores = lax.dot_general(logged, queries, (((1,), (1,)), ((), ())), preferred_element_type=jnp.float32)
    return logged, scores
```

```python
import functools

import jax
import jax.numpy as jnp
from jax import lax
from jax.experimental import pallas as pl
from jax.experimental.pallas import tpu as pltpu
from jax.sharding import PartitionSpec as P

MIB = 1 << 20
ROWS = (((1,), (1,)), ((), ()))


def outer_grads(left_rows, right_rows, ex_dev, seq_len, layers, proj_rank):
    left_wide = left_rows.astype(jnp.float32).reshape(ex_dev, seq_len, layers, proj_rank)
    right_wide = right_rows.reshape(ex_dev, seq_len, layers, proj_rank)
    return jnp.einsum("esli,eslj->elij", left_wide, right_wide, precision=lax.Precision.HIGH)


def on_any_mesh(inputs, out_grads, lengths, proj_in, proj_out, queries):
    layers = inputs.shape[0]
    tok_dev = inputs.shape[1]
    ex_dev = lengths.shape[0]
    seq_len = tok_dev // ex_dev
    proj_rank = proj_in.shape[2]
    shard_count = lax.axis_size("mp")
    tok_mp = tok_dev // shard_count
    row_base = lax.axis_index("mp") * tok_mp
    row_ids = row_base + jnp.arange(tok_mp, dtype=jnp.int32)
    owners = row_ids // seq_len
    within = row_ids % seq_len
    limits = jnp.sum(
        jnp.where(
            owners[:, None] == jnp.arange(ex_dev, dtype=jnp.int32)[None, :], lengths[None, :], 0
        ),
        axis=1,
    )
    is_live = within < limits
    projected = jnp.concatenate(
        [
            jnp.dot(out_grads[layer_idx], proj_out[layer_idx], preferred_element_type=jnp.float32)
            for layer_idx in range(layers)
        ],
        axis=1,
    )
    outer_side = jnp.where(is_live[:, None], projected, jnp.float32(0.0)).astype(jnp.bfloat16)
    outer_side = lax.optimization_barrier(outer_side)
    pieces = [
        jnp.dot(inputs[layer_idx], proj_in[layer_idx], preferred_element_type=jnp.float32)
        for layer_idx in range(layers)
    ]
    local_side = jnp.concatenate(pieces, axis=1)
    gathered = lax.all_gather(outer_side, "mp", axis=0, tiled=True)
    grads = outer_grads(gathered, local_side, ex_dev, seq_len, layers, proj_rank)
    flat_grads = grads.reshape(ex_dev, layers * proj_rank * proj_rank)
    my_share = lax.psum_scatter(flat_grads, "mp", scatter_dimension=1, tiled=True)
    logged = my_share.astype(jnp.bfloat16)
    everyone = lax.all_gather(logged, "example", axis=0, tiled=True)
    score_part = lax.dot_general(
        everyone, queries, (((1,), (1,)), ((), ())), preferred_element_type=jnp.float32
    )
    partial_scores = lax.all_to_all(score_part, "example", split_axis=0, concat_axis=1, tiled=True)
    scores = lax.psum(partial_scores, "mp")
    return (logged, scores)


def project_kernel(lens, x_hbm, w_hbm, o_ref, xbuf, wbuf, blocks, xsem, wsem, *, seq, masked):
    layers, rows, _ = x_hbm.shape
    slots, bt, _ = xbuf.shape
    half = bt // 2
    base = lax.axis_index("mp") * rows if masked else 0

    def live_in(block):
        row = base + block * bt
        return lens[lax.div(row, seq)] - lax.rem(row, seq)

    def add(block, count):
        live = live_in(block) > 0

        @pl.when(live)
        def _():
            blocks[count] = block

        return count + live.astype(jnp.int32)

    count = lax.fori_loop(0, rows // bt, add, jnp.int32(0))
    total = count * layers

    def place(item):
        layer = lax.div(item, count)
        return layer, blocks[item - layer * count]

    def piece(layer, block, slot, part):
        row = pl.multiple_of(block * bt + part * half, half)
        return pltpu.make_async_copy(
            x_hbm.at[layer, pl.ds(row, half)],
            xbuf.at[slot, pl.ds(part * half, half)],
            xsem.at[slot, part],
        )

    def fetch(item):
        layer, block = place(item)
        slot = lax.rem(item, slots)
        piece(layer, block, slot, 0).start()

        @pl.when(live_in(block) > half)
        def _():
            piece(layer, block, slot, 1).start()

    def weight(layer):
        return pltpu.make_async_copy(w_hbm.at[layer], wbuf.at[layer], wsem.at[layer])

    weight(0).start()
    for item in range(slots):

        @pl.when(item < total)
        def _():
            fetch(jnp.int32(item))

        if item == 0:
            for layer in range(1, layers):
                weight(layer).start()

    o_ref[...] = jnp.zeros_like(o_ref)

    def compute(layer, block, slot, width):
        out = lax.dot_general(
            wbuf[layer], xbuf[slot, :width], ROWS, preferred_element_type=jnp.float32
        )
        if masked:
            at = lax.broadcasted_iota(jnp.int32, out.shape, 1)
            out = jnp.where(at < live_in(block), out, 0.0)
        col = pl.multiple_of(block * bt, bt)
        o_ref[layer, :, pl.ds(col, width)] = out.astype(o_ref.dtype)

    def step(item, carry):
        layer, block = place(item)
        slot = lax.rem(item, slots)
        wide = live_in(block) > half

        for at in range(layers):

            @pl.when(item == at * count)
            def _():
                weight(at).wait()

        piece(layer, block, slot, 0).wait()

        @pl.when(wide)
        def _():
            piece(layer, block, slot, 1).wait()
            compute(layer, block, slot, bt)

        @pl.when(jnp.logical_not(wide))
        def _():
            compute(layer, block, slot, half)

        @pl.when(item + slots < total)
        def _():
            fetch(item + slots)

        return carry

    lax.fori_loop(0, total, step, 0)

    @pl.when(count == 0)
    def _():
        for layer in range(layers):
            weight(layer).wait()


def project(lengths, x, w, seq, masked, bt, slots, dtype):
    layers, rows, depth = x.shape
    rank = w.shape[1]
    return pl.pallas_call(
        functools.partial(project_kernel, seq=seq, masked=masked),
        out_shape=jax.ShapeDtypeStruct((layers, rank, rows), dtype),
        in_specs=[
            pl.BlockSpec(memory_space=pltpu.SMEM),
            pl.BlockSpec(memory_space=pltpu.HBM),
            pl.BlockSpec(memory_space=pltpu.HBM),
        ],
        out_specs=pl.BlockSpec(memory_space=pltpu.VMEM),
        scratch_shapes=[
            pltpu.VMEM((slots, bt, depth), x.dtype),
            pltpu.VMEM((layers, rank, depth), w.dtype),
            pltpu.SMEM((rows // bt,), jnp.int32),
            pltpu.SemaphoreType.DMA((slots, 2)),
            pltpu.SemaphoreType.DMA((layers,)),
        ],
        compiler_params=pltpu.CompilerParams(vmem_limit_bytes=32 * MIB),
        cost_estimate=pl.CostEstimate(
            flops=2 * layers * rows * depth * 256, bytes_accessed=x.size * 2, transcendentals=0
        ),
    )(lengths, x, w)


def grads_kernel(x_ref, *refs, count, seq):
    outer, outs, (all_outer, square, cut) = refs[:count], refs[count : 2 * count], refs[2 * count :]
    layers, rank, tokens = x_ref.shape
    width = outer[0].shape[2]
    me = lax.axis_index("mp")
    for k in range(count):
        at = pl.multiple_of(lax.bitwise_xor(me, k) * width, width)
        all_outer[:, :, pl.ds(at, width)] = outer[k][...]
    share_rows = cut.shape[2]
    left = lax.broadcasted_iota(jnp.int32, (rank // 2, 2 * rank), 1) < rank
    for e in range(tokens // seq):
        for layer in range(layers):
            x = x_ref[layer, :, e * seq : (e + 1) * seq]
            high = x.astype(jnp.bfloat16)
            low = (x - high.astype(jnp.float32)).astype(jnp.bfloat16)
            o = all_outer[layer, :, e * seq : (e + 1) * seq]
            both = [
                lax.dot_general(
                    o, jnp.concatenate([part, part], 0), ROWS, preferred_element_type=jnp.float32
                )
                for part in (high, low)
            ]
            at = e * layers + layer
            square[at] = both[0] + both[1]
            even = square[at, pl.ds(0, rank // 2, stride=2), :]
            odd = square[at, pl.ds(1, rank // 2, stride=2), :]
            flat = jnp.where(left, even, odd)
            for row in range(0, rank // 2, share_rows):
                share = (layer * (rank // 2) + row) // share_rows
                cut[share, e] = flat[row : row + share_rows]
    for k in range(count):
        outs[k][...] = cut[lax.bitwise_xor(me, k)]


def grads_shares(x, outer, ex_dev, seq):
    layers, rank, tokens = x.shape
    count = len(outer)
    share = (ex_dev, layers * rank * rank // count // 128, 128)
    return pl.pallas_call(
        functools.partial(grads_kernel, count=count, seq=seq),
        out_shape=[jax.ShapeDtypeStruct(share, jnp.float32)] * count,
        in_specs=[pl.BlockSpec(memory_space=pltpu.VMEM)] * (count + 1),
        out_specs=[pl.BlockSpec(memory_space=pltpu.VMEM)] * count,
        scratch_shapes=[
            pltpu.VMEM((layers, rank, tokens), jnp.bfloat16),
            pltpu.VMEM((ex_dev * layers, rank, 2 * rank), jnp.float32),
            pltpu.VMEM((count, *share), jnp.float32),
        ],
        compiler_params=pltpu.CompilerParams(vmem_limit_bytes=24 * MIB),
        cost_estimate=pl.CostEstimate(flops=10**9, bytes_accessed=4 * MIB, transcendentals=0),
    )(x, *outer)


def scores_kernel(*refs, shares, parts):
    share_refs, query_refs = refs[:shares], refs[shares : shares + parts]
    logged_ref, part_ref, flat = refs[shares + parts :]
    ex_dev, rows, lanes = share_refs[0].shape
    me = lax.axis_index("example")
    sums = [ref[...] for ref in share_refs]
    while len(sums) > 1:
        sums = [a + b for a, b in zip(sums[::2], sums[1::2])]
    flat[...] = jnp.zeros_like(flat)
    for e in range(ex_dev):
        for row in range(rows):
            flat[e : e + 1, row * lanes : (row + 1) * lanes] = sums[0][e, row : row + 1, :]
    rounded = flat[...].astype(jnp.bfloat16)
    logged_ref[...] = rounded[:ex_dev]
    width = query_refs[0].shape[0]
    for k in range(parts):
        out = lax.dot_general(rounded, query_refs[k][...], ROWS, preferred_element_type=jnp.float32)
        at = pl.multiple_of(lax.bitwise_xor(me, k) * width, width)
        part_ref[:, pl.ds(at, width)] = out[:ex_dev]


def logged_and_part(shares, queries):
    ex_dev, rows, lanes = shares[0].shape
    width = queries[0].shape[0] * len(queries)
    return pl.pallas_call(
        functools.partial(scores_kernel, shares=len(shares), parts=len(queries)),
        out_shape=[
            jax.ShapeDtypeStruct((ex_dev, rows * lanes), jnp.bfloat16),
            jax.ShapeDtypeStruct((ex_dev, width), jnp.float32),
        ],
        in_specs=[pl.BlockSpec(memory_space=pltpu.VMEM)] * (len(shares) + len(queries)),
        out_specs=[pl.BlockSpec(memory_space=pltpu.VMEM)] * 2,
        scratch_shapes=[pltpu.VMEM((16, rows * lanes), jnp.float32)],
        compiler_params=pltpu.CompilerParams(vmem_limit_bytes=24 * MIB),
        cost_estimate=pl.CostEstimate(flops=10**9, bytes_accessed=5 * MIB, transcendentals=0),
    )(*shares, *queries)


def swap(x, axis, k):
    return lax.ppermute(x, axis, [(i, i ^ k) for i in range(lax.axis_size(axis))])


def on_device(inputs, out_grads, lengths, proj_in, proj_out, queries):
    ex_dev = lengths.shape[0]
    seq = inputs.shape[1] // ex_dev
    mp = lax.axis_size("mp")
    across = swap(queries, "example", 2)
    mine = project(
        lengths, out_grads, jnp.swapaxes(proj_out, 1, 2), seq, True, 256, 3, jnp.bfloat16
    )
    mine, later = lax.optimization_barrier((mine, lengths))
    outer = [mine] + [swap(mine, "mp", k) for k in range(1, mp)]
    x = project(later, inputs, jnp.swapaxes(proj_in, 1, 2), seq, False, 256, 4, jnp.float32)
    shares = grads_shares(x, outer, ex_dev, seq)
    shares, across = lax.optimization_barrier((shares, across))
    all_queries = [queries, swap(queries, "example", 1), across, swap(across, "example", 1)]
    shares = [shares[0]] + [swap(shares[k], "mp", k) for k in range(1, mp)]
    logged, part = logged_and_part(shares, all_queries)
    parts = [part] + [swap(part, "mp", k) for k in range(1, mp)]
    scores = (parts[0] + parts[1]) + (parts[2] + parts[3])
    return logged, scores


def kernels_fit(inputs, out_grads, lengths, proj_in, mesh):
    shape = dict(mesh.shape)
    split = shape["groups"] * shape["example"]
    tokens, examples = inputs.shape[1] // split, lengths.shape[0] // split
    return (
        shape["mp"] == 4
        and shape["example"] == 4
        and inputs.shape[0] == 2
        and proj_in.shape[2] == 64
        and examples <= 16
        and (tokens // examples) % 256 == 0
        and (tokens // 4) % 256 == 0
    )


def solution(mesh):
    placed = (
        P(None, ("groups", "example"), "mp"),
        P(None, ("groups", "example", "mp"), None),
        P(("groups", "example")),
        P(None, "mp", None),
        P(),
        P("example", "mp"),
    )

    def whole(inputs, out_grads, lengths, proj_in, proj_out, queries):
        fit = kernels_fit(inputs, out_grads, lengths, proj_in, mesh)
        return jax.shard_map(
            on_device if fit else on_any_mesh,
            mesh=mesh,
            in_specs=placed,
            out_specs=(P(("groups", "example"), "mp"), P(("groups", "example"), None)),
            check_vma=False,
        )(inputs, out_grads, lengths, proj_in, proj_out, queries)

    return whole
```

```python
import functools

import jax
import jax.numpy as jnp
from jax import lax
from jax.experimental import pallas as pl
from jax.experimental.pallas import tpu as pltpu
from jax.sharding import PartitionSpec as P

MIB = 1 << 20
ROWS = (((1,), (1,)), ((), ()))


def outer_grads(left_rows, right_rows, ex_dev, seq_len, layers, proj_rank):
    left_wide = left_rows.astype(jnp.float32).reshape(ex_dev, seq_len, layers, proj_rank)
    right_wide = right_rows.reshape(ex_dev, seq_len, layers, proj_rank)
    return jnp.einsum("esli,eslj->elij", left_wide, right_wide, precision=lax.Precision.HIGH)


def on_any_mesh(inputs, out_grads, lengths, proj_in, proj_out, queries):
    layers = inputs.shape[0]
    tok_dev = inputs.shape[1]
    ex_dev = lengths.shape[0]
    seq_len = tok_dev // ex_dev
    proj_rank = proj_in.shape[2]
    shard_count = lax.axis_size("mp")
    tok_mp = tok_dev // shard_count
    row_base = lax.axis_index("mp") * tok_mp
    row_ids = row_base + jnp.arange(tok_mp, dtype=jnp.int32)
    owners = row_ids // seq_len
    within = row_ids % seq_len
    limits = jnp.sum(
        jnp.where(
            owners[:, None] == jnp.arange(ex_dev, dtype=jnp.int32)[None, :], lengths[None, :], 0
        ),
        axis=1,
    )
    is_live = within < limits
    projected = jnp.concatenate(
        [
            jnp.dot(out_grads[layer_idx], proj_out[layer_idx], preferred_element_type=jnp.float32)
            for layer_idx in range(layers)
        ],
        axis=1,
    )
    outer_side = jnp.where(is_live[:, None], projected, jnp.float32(0.0)).astype(jnp.bfloat16)
    outer_side = lax.optimization_barrier(outer_side)
    pieces = [
        jnp.dot(inputs[layer_idx], proj_in[layer_idx], preferred_element_type=jnp.float32)
        for layer_idx in range(layers)
    ]
    local_side = jnp.concatenate(pieces, axis=1)
    gathered = lax.all_gather(outer_side, "mp", axis=0, tiled=True)
    grads = outer_grads(gathered, local_side, ex_dev, seq_len, layers, proj_rank)
    flat_grads = grads.reshape(ex_dev, layers * proj_rank * proj_rank)
    my_share = lax.psum_scatter(flat_grads, "mp", scatter_dimension=1, tiled=True)
    logged = my_share.astype(jnp.bfloat16)
    everyone = lax.all_gather(logged, "example", axis=0, tiled=True)
    score_part = lax.dot_general(
        everyone, queries, (((1,), (1,)), ((), ())), preferred_element_type=jnp.float32
    )
    partial_scores = lax.all_to_all(score_part, "example", split_axis=0, concat_axis=1, tiled=True)
    scores = lax.psum(partial_scores, "mp")
    return (logged, scores)


def project_kernel(lens_hbm, x_hbm, w_hbm, o_ref, xbuf, wbuf, sums, lens, places, xsem, wsem, lsem, *, seq, masked):
    layers, rows, _ = x_hbm.shape
    rank = w_hbm.shape[1]
    slots, chunk, _ = xbuf.shape
    most = xsem.shape[1]
    granule = chunk // most
    half = most // 2
    base = lax.axis_index("mp") * rows if masked else 0

    lens_copy = pltpu.make_async_copy(lens_hbm, lens, lsem)
    lens_copy.start()
    weights = [
        pltpu.make_async_copy(w_hbm.at[layer], wbuf.at[pl.ds(layer * rank, rank)], wsem.at[layer])
        for layer in range(layers)
    ]
    for copy in weights:
        copy.start()
    lens_copy.wait()

    spans = []
    count = jnp.int32(0)
    for e in range(lens.shape[0]):
        low = jnp.clip(e * seq - base, 0, rows)
        high = jnp.clip(e * seq + lens[e] - base, 0, rows)
        here = lax.shift_right_logical(jnp.maximum(high - low, 0) + (granule - 1), granule.bit_length() - 1)

        def put(i, carry, low=low, at=count):
            places[at + i] = low + i * granule
            return carry

        lax.fori_loop(0, here, put, 0)
        count = count + here
        spans.append((low, high))
    total = count * layers

    def place(item):
        layer = (item >= count).astype(jnp.int32)
        return layer, pl.multiple_of(places[item - layer * count], granule)

    def in_chunk(c):
        first = jnp.maximum(c * most - half, 0)
        return first, jnp.minimum(jnp.where(c == 0, half, most), total - first)

    chunks = lax.shift_right_logical(total + half + most - 1, most.bit_length() - 1)
    chunks = jnp.where(total > 0, chunks, 0)

    def piece(item, slot, g):
        layer, row = place(item)
        return pltpu.make_async_copy(
            x_hbm.at[layer, pl.ds(row, granule)],
            xbuf.at[slot, pl.ds(g * granule, granule)],
            xsem.at[slot, g],
        )

    def each(c, slot, start):
        first, n = in_chunk(c)
        for g in range(most):

            @pl.when(g < n)
            def _():
                copy = piece(first + g, slot, g)
                copy.start() if start else copy.wait()

    for c in range(slots):

        @pl.when(c < chunks)
        def _():
            each(jnp.int32(c), c, True)

    sums[...] = jnp.zeros_like(sums)
    for copy in weights:
        copy.wait()
    second = lax.broadcasted_iota(jnp.int32, (granule, layers * rank), 1) // rank

    def compute(c, slot, parts):
        first, n = in_chunk(c)
        out = lax.dot_general(
            xbuf[slot, : parts * granule], wbuf[...], ROWS, preferred_element_type=jnp.float32
        )
        for g in range(parts):
            layer, row = place(jnp.minimum(first + g, total - 1))
            row = pl.multiple_of(jnp.where(g < n, row, rows), granule)
            at = pl.ds(row, granule)
            sums[at, :] = jnp.where(second == layer, out[g * granule : (g + 1) * granule], sums[at, :])

    def step(c, slot):
        each(c, slot, False)
        n = in_chunk(c)[1]
        pl.when(n <= half)(functools.partial(compute, c, slot, half))
        pl.when(n > half)(functools.partial(compute, c, slot, most))

        @pl.when(c + slots < chunks)
        def _():
            each(c + slots, slot, True)

        return jnp.where(slot + 1 == slots, 0, slot + 1)

    lax.fori_loop(0, chunks, step, jnp.int32(0))
    if masked:
        turned = sums[:rows].T
        token = lax.broadcasted_iota(jnp.int32, turned.shape, 1)
        live = token < 0
        for low, high in spans:
            live = live | ((token >= low) & (token < high))
        o_ref[...] = jnp.where(live, turned, 0.0).astype(o_ref.dtype)


def project(lengths, x, w, seq, masked, chunk, granule, slots, limit):
    layers, rows, depth = x.shape
    rank = w.shape[1]
    wide = layers * rank
    summed = (rows + granule, wide)
    if masked:
        out = jax.ShapeDtypeStruct((wide, rows), jnp.bfloat16)
        body = project_kernel
        more = [pltpu.VMEM(summed, jnp.float32)]
    else:
        out = jax.ShapeDtypeStruct(summed, jnp.float32)
        more = []

        def body(lens_hbm, x_hbm, w_hbm, o_ref, xbuf, wbuf, *rest, **options):
            project_kernel(lens_hbm, x_hbm, w_hbm, o_ref, xbuf, wbuf, o_ref, *rest, **options)

    return pl.pallas_call(
        functools.partial(body, seq=seq, masked=masked),
        out_shape=out,
        in_specs=[pl.BlockSpec(memory_space=pltpu.HBM)] * 3,
        out_specs=pl.BlockSpec(memory_space=pltpu.VMEM),
        scratch_shapes=[
            pltpu.VMEM((slots, chunk, depth), x.dtype),
            pltpu.VMEM((wide, depth), w.dtype),
            *more,
            pltpu.SMEM(lengths.shape, jnp.int32),
            pltpu.SMEM((rows // granule,), jnp.int32),
            pltpu.SemaphoreType.DMA((slots, chunk // granule)),
            pltpu.SemaphoreType.DMA((layers,)),
            pltpu.SemaphoreType.DMA,
        ],
        compiler_params=pltpu.CompilerParams(vmem_limit_bytes=limit * MIB),
        cost_estimate=pl.CostEstimate(
            flops=2 * layers * rows * depth * 256, bytes_accessed=x.size * 2, transcendentals=0
        ),
    )(lengths, x, w)


def grads_kernel(x_ref, *refs, count, seq):
    outer, outs, (all_outer, square, cut) = refs[:count], refs[count : 2 * count], refs[2 * count :]
    wide, width = outer[0].shape
    examples, rank = cut.shape[1], wide // 2
    me = lax.axis_index("mp")
    for k in range(count):
        at = pl.multiple_of(lax.bitwise_xor(me, k) * width, width)
        all_outer[:, pl.ds(at, width)] = outer[k][...]
    share_rows = cut.shape[2]
    left = lax.broadcasted_iota(jnp.int32, (rank // 2, wide), 1) < rank
    for e in range(examples):
        x = x_ref[e * seq : (e + 1) * seq, :]
        high = x.astype(jnp.bfloat16)
        low = (x - high.astype(jnp.float32)).astype(jnp.bfloat16)
        o = all_outer[:, e * seq : (e + 1) * seq]
        square[e] = jnp.dot(o, high, preferred_element_type=jnp.float32) + jnp.dot(
            o, low, preferred_element_type=jnp.float32
        )
        for layer in range(2):
            even = square[e, pl.ds(layer * rank, rank // 2, stride=2), :]
            odd = square[e, pl.ds(layer * rank + 1, rank // 2, stride=2), :]
            if layer == 0:
                odd = pltpu.roll(odd, rank, 1)
            else:
                even = pltpu.roll(even, rank, 1)
            flat = jnp.where(left, even, odd)
            for row in range(0, rank // 2, share_rows):
                share = (layer * (rank // 2) + row) // share_rows
                cut[share, e] = flat[row : row + share_rows]
    for k in range(count):
        outs[k][...] = cut[lax.bitwise_xor(me, k)]


def grads_shares(x, outer, ex_dev, seq):
    wide = x.shape[1]
    count = len(outer)
    share = (ex_dev, wide * wide // 2 // count // 128, 128)
    return pl.pallas_call(
        functools.partial(grads_kernel, count=count, seq=seq),
        out_shape=[jax.ShapeDtypeStruct(share, jnp.float32)] * count,
        in_specs=[pl.BlockSpec(memory_space=pltpu.VMEM)] * (count + 1),
        out_specs=[pl.BlockSpec(memory_space=pltpu.VMEM)] * count,
        scratch_shapes=[
            pltpu.VMEM((wide, ex_dev * seq), jnp.bfloat16),
            pltpu.VMEM((ex_dev, wide, wide), jnp.float32),
            pltpu.VMEM((count, *share), jnp.float32),
        ],
        compiler_params=pltpu.CompilerParams(vmem_limit_bytes=16 * MIB),
        cost_estimate=pl.CostEstimate(flops=10**9, bytes_accessed=4 * MIB, transcendentals=0),
    )(x, *outer)


def scores_kernel(*refs, shares, parts):
    share_refs, query_refs = refs[:shares], refs[shares : shares + parts]
    logged_ref, part_ref, flat = refs[shares + parts :]
    ex_dev, rows, lanes = share_refs[0].shape
    me = lax.axis_index("example")
    sums = [ref[...] for ref in share_refs]
    while len(sums) > 1:
        sums = [a + b for a, b in zip(sums[::2], sums[1::2])]
    flat[...] = jnp.zeros_like(flat)
    for e in range(ex_dev):
        for row in range(rows):
            flat[e : e + 1, row * lanes : (row + 1) * lanes] = sums[0][e, row : row + 1, :]
    rounded = flat[...].astype(jnp.bfloat16)
    logged_ref[...] = rounded[:ex_dev]
    width = query_refs[0].shape[0]
    for k in range(parts):
        out = lax.dot_general(rounded, query_refs[k][...], ROWS, preferred_element_type=jnp.float32)
        at = pl.multiple_of(lax.bitwise_xor(me, k) * width, width)
        part_ref[:, pl.ds(at, width)] = out[:ex_dev]


def logged_and_part(shares, queries):
    ex_dev, rows, lanes = shares[0].shape
    width = queries[0].shape[0] * len(queries)
    return pl.pallas_call(
        functools.partial(scores_kernel, shares=len(shares), parts=len(queries)),
        out_shape=[
            jax.ShapeDtypeStruct((ex_dev, rows * lanes), jnp.bfloat16),
            jax.ShapeDtypeStruct((ex_dev, width), jnp.float32),
        ],
        in_specs=[pl.BlockSpec(memory_space=pltpu.VMEM)] * (len(shares) + len(queries)),
        out_specs=[pl.BlockSpec(memory_space=pltpu.VMEM)] * 2,
        scratch_shapes=[pltpu.VMEM((16, rows * lanes), jnp.float32)],
        compiler_params=pltpu.CompilerParams(vmem_limit_bytes=24 * MIB),
        cost_estimate=pl.CostEstimate(flops=10**9, bytes_accessed=5 * MIB, transcendentals=0),
    )(*shares, *queries)


def swap(x, axis, k):
    return lax.ppermute(x, axis, [(i, i ^ k) for i in range(lax.axis_size(axis))])


def on_device(inputs, out_grads, lengths, proj_in, proj_out, queries):
    ex_dev = lengths.shape[0]
    seq = inputs.shape[1] // ex_dev
    mp = lax.axis_size("mp")
    across = swap(queries, "example", 2)
    mine = project(lengths, out_grads, jnp.swapaxes(proj_out, 1, 2), seq, True, 256, 64, 3, 60)
    mine, later = lax.optimization_barrier((mine, lengths))
    outer = [mine] + [swap(mine, "mp", k) for k in range(1, mp)]
    x = project(later, inputs, jnp.swapaxes(proj_in, 1, 2), seq, False, 512, 64, 3, 32)
    x, across, *outer = lax.optimization_barrier((x, across, *outer))
    all_queries = [queries, swap(queries, "example", 1), across, swap(across, "example", 1)]
    shares = grads_shares(x, outer, ex_dev, seq)
    shares = [shares[0]] + [swap(shares[k], "mp", k) for k in range(1, mp)]
    logged, part = logged_and_part(shares, all_queries)
    parts = [part] + [swap(part, "mp", k) for k in range(1, mp)]
    scores = (parts[0] + parts[1]) + (parts[2] + parts[3])
    return logged, scores


def kernels_fit(inputs, out_grads, lengths, proj_in, mesh):
    shape = dict(mesh.shape)
    split = shape["groups"] * shape["example"]
    tokens, examples = inputs.shape[1] // split, lengths.shape[0] // split
    return (
        shape["mp"] == 4
        and shape["example"] == 4
        and inputs.shape[0] == 2
        and proj_in.shape[2] == 64
        and examples <= 16
        and (tokens // examples) % 256 == 0
        and (tokens // 4) % 256 == 0
    )


def solution(mesh):
    placed = (
        P(None, ("groups", "example"), "mp"),
        P(None, ("groups", "example", "mp"), None),
        P(("groups", "example")),
        P(None, "mp", None),
        P(),
        P("example", "mp"),
    )

    def whole(inputs, out_grads, lengths, proj_in, proj_out, queries):
        fit = kernels_fit(inputs, out_grads, lengths, proj_in, mesh)
        return jax.shard_map(
            on_device if fit else on_any_mesh,
            mesh=mesh,
            in_specs=placed,
            out_specs=(P(("groups", "example"), "mp"), P(("groups", "example"), None)),
            check_vma=False,
        )(inputs, out_grads, lengths, proj_in, proj_out, queries)

    return whole
```

```python
import functools

import jax
import jax.numpy as jnp
from jax import lax
from jax.experimental import pallas as pl
from jax.experimental.pallas import tpu as pltpu
from jax.sharding import PartitionSpec as P

MIB = 1 << 20
ROWS = (((1,), (1,)), ((), ()))


def outer_grads(left_rows, right_rows, ex_dev, seq_len, layers, proj_rank):
    left_wide = left_rows.astype(jnp.float32).reshape(ex_dev, seq_len, layers, proj_rank)
    right_wide = right_rows.reshape(ex_dev, seq_len, layers, proj_rank)
    return jnp.einsum("esli,eslj->elij", left_wide, right_wide, precision=lax.Precision.HIGH)


def on_any_mesh(inputs, out_grads, lengths, proj_in, proj_out, queries):
    layers = inputs.shape[0]
    tok_dev = inputs.shape[1]
    ex_dev = lengths.shape[0]
    seq_len = tok_dev // ex_dev
    proj_rank = proj_in.shape[2]
    shard_count = lax.axis_size("mp")
    tok_mp = tok_dev // shard_count
    row_base = lax.axis_index("mp") * tok_mp
    row_ids = row_base + jnp.arange(tok_mp, dtype=jnp.int32)
    owners = row_ids // seq_len
    within = row_ids % seq_len
    limits = jnp.sum(
        jnp.where(
            owners[:, None] == jnp.arange(ex_dev, dtype=jnp.int32)[None, :], lengths[None, :], 0
        ),
        axis=1,
    )
    is_live = within < limits
    projected = jnp.concatenate(
        [
            jnp.dot(out_grads[layer_idx], proj_out[layer_idx], preferred_element_type=jnp.float32)
            for layer_idx in range(layers)
        ],
        axis=1,
    )
    outer_side = jnp.where(is_live[:, None], projected, jnp.float32(0.0)).astype(jnp.bfloat16)
    outer_side = lax.optimization_barrier(outer_side)
    pieces = [
        jnp.dot(inputs[layer_idx], proj_in[layer_idx], preferred_element_type=jnp.float32)
        for layer_idx in range(layers)
    ]
    local_side = jnp.concatenate(pieces, axis=1)
    gathered = lax.all_gather(outer_side, "mp", axis=0, tiled=True)
    grads = outer_grads(gathered, local_side, ex_dev, seq_len, layers, proj_rank)
    flat_grads = grads.reshape(ex_dev, layers * proj_rank * proj_rank)
    my_share = lax.psum_scatter(flat_grads, "mp", scatter_dimension=1, tiled=True)
    logged = my_share.astype(jnp.bfloat16)
    everyone = lax.all_gather(logged, "example", axis=0, tiled=True)
    score_part = lax.dot_general(
        everyone, queries, (((1,), (1,)), ((), ())), preferred_element_type=jnp.float32
    )
    partial_scores = lax.all_to_all(score_part, "example", split_axis=0, concat_axis=1, tiled=True)
    scores = lax.psum(partial_scores, "mp")
    return (logged, scores)


def project_kernel(lens_hbm, x_hbm, w_hbm, o_ref, xbuf, wbuf, sums, lens, places, xsem, wsem, lsem, *, seq, masked):
    layers, rows, _ = x_hbm.shape
    rank = w_hbm.shape[1]
    slots, chunk, _ = xbuf.shape
    most = xsem.shape[1]
    granule = chunk // most
    half = most // 2
    base = lax.axis_index("mp") * rows if masked else 0

    lens_copy = pltpu.make_async_copy(lens_hbm, lens, lsem)
    lens_copy.start()
    weights = [
        pltpu.make_async_copy(w_hbm.at[layer], wbuf.at[pl.ds(layer * rank, rank)], wsem.at[layer])
        for layer in range(layers)
    ]
    for copy in weights:
        copy.start()
    lens_copy.wait()

    spans = []
    count = jnp.int32(0)
    for e in range(lens.shape[0]):
        low = jnp.clip(e * seq - base, 0, rows)
        high = jnp.clip(e * seq + lens[e] - base, 0, rows)
        here = lax.shift_right_logical(jnp.maximum(high - low, 0) + (granule - 1), granule.bit_length() - 1)

        def put(i, carry, low=low, at=count):
            places[at + i] = low + i * granule
            return carry

        lax.fori_loop(0, here, put, 0)
        count = count + here
        spans.append((low, high))
    total = count * layers

    def place(item):
        layer = (item >= count).astype(jnp.int32)
        return layer, pl.multiple_of(places[item - layer * count], granule)

    def in_chunk(c):
        first = jnp.maximum(c * most - half, 0)
        return first, jnp.minimum(jnp.where(c == 0, half, most), total - first)

    chunks = lax.shift_right_logical(total + half + most - 1, most.bit_length() - 1)
    chunks = jnp.where(total > 0, chunks, 0)

    def piece(item, slot, g):
        layer, row = place(item)
        return pltpu.make_async_copy(
            x_hbm.at[layer, pl.ds(row, granule)],
            xbuf.at[slot, pl.ds(g * granule, granule)],
            xsem.at[slot, g],
        )

    def each(c, slot, start):
        first, n = in_chunk(c)
        for g in range(most):

            @pl.when(g < n)
            def _():
                copy = piece(first + g, slot, g)
                copy.start() if start else copy.wait()

    for c in range(slots):

        @pl.when(c < chunks)
        def _():
            each(jnp.int32(c), c, True)

    sums[...] = jnp.zeros_like(sums)
    for copy in weights:
        copy.wait()
    second = lax.broadcasted_iota(jnp.int32, (granule, layers * rank), 1) // rank

    def compute(c, slot, parts):
        first, n = in_chunk(c)
        out = lax.dot_general(
            xbuf[slot, : parts * granule], wbuf[...], ROWS, preferred_element_type=jnp.float32
        )
        for g in range(parts):
            layer, row = place(jnp.minimum(first + g, total - 1))
            row = pl.multiple_of(jnp.where(g < n, row, rows), granule)
            at = pl.ds(row, granule)
            sums[at, :] = jnp.where(second == layer, out[g * granule : (g + 1) * granule], sums[at, :])

    def step(c, slot):
        each(c, slot, False)
        n = in_chunk(c)[1]
        pl.when(n <= half)(functools.partial(compute, c, slot, half))
        pl.when(n > half)(functools.partial(compute, c, slot, most))

        @pl.when(c + slots < chunks)
        def _():
            each(c + slots, slot, True)

        return jnp.where(slot + 1 == slots, 0, slot + 1)

    lax.fori_loop(0, chunks, step, jnp.int32(0))
    if masked:
        turned = sums[:rows].T
        token = lax.broadcasted_iota(jnp.int32, turned.shape, 1)
        live = token < 0
        for low, high in spans:
            live = live | ((token >= low) & (token < high))
        o_ref[...] = jnp.where(live, turned, 0.0).astype(o_ref.dtype)


def project(lengths, x, w, seq, masked, chunk, granule, slots, limit):
    layers, rows, depth = x.shape
    rank = w.shape[1]
    wide = layers * rank
    summed = (rows + granule, wide)
    if masked:
        out = jax.ShapeDtypeStruct((wide, rows), jnp.bfloat16)
        body = project_kernel
        more = [pltpu.VMEM(summed, jnp.float32)]
    else:
        out = jax.ShapeDtypeStruct(summed, jnp.float32)
        more = []

        def body(lens_hbm, x_hbm, w_hbm, o_ref, xbuf, wbuf, *rest, **options):
            project_kernel(lens_hbm, x_hbm, w_hbm, o_ref, xbuf, wbuf, o_ref, *rest, **options)

    return pl.pallas_call(
        functools.partial(body, seq=seq, masked=masked),
        out_shape=out,
        in_specs=[pl.BlockSpec(memory_space=pltpu.HBM)] * 3,
        out_specs=pl.BlockSpec(memory_space=pltpu.VMEM),
        scratch_shapes=[
            pltpu.VMEM((slots, chunk, depth), x.dtype),
            pltpu.VMEM((wide, depth), w.dtype),
            *more,
            pltpu.SMEM(lengths.shape, jnp.int32),
            pltpu.SMEM((rows // granule,), jnp.int32),
            pltpu.SemaphoreType.DMA((slots, chunk // granule)),
            pltpu.SemaphoreType.DMA((layers,)),
            pltpu.SemaphoreType.DMA,
        ],
        compiler_params=pltpu.CompilerParams(vmem_limit_bytes=limit * MIB),
        cost_estimate=pl.CostEstimate(
            flops=layers * rows * depth * 16, bytes_accessed=x.size // 8, transcendentals=0
        ),
    )(lengths, x, w)


def grads_kernel(x_ref, *refs, count, seq):
    outer, outs, (all_outer, square, cut) = refs[:count], refs[count : 2 * count], refs[2 * count :]
    wide, width = outer[0].shape
    examples, rank = cut.shape[1], wide // 2
    me = lax.axis_index("mp")
    for k in range(count):
        at = pl.multiple_of(lax.bitwise_xor(me, k) * width, width)
        all_outer[:, pl.ds(at, width)] = outer[k][...]
    share_rows = cut.shape[2]
    left = lax.broadcasted_iota(jnp.int32, (rank // 2, wide), 1) < rank
    for e in range(examples):
        x = x_ref[e * seq : (e + 1) * seq, :]
        high = x.astype(jnp.bfloat16)
        low = (x - high.astype(jnp.float32)).astype(jnp.bfloat16)
        o = all_outer[:, e * seq : (e + 1) * seq]
        square[e] = jnp.dot(o, high, preferred_element_type=jnp.float32) + jnp.dot(
            o, low, preferred_element_type=jnp.float32
        )
        for layer in range(2):
            even = square[e, pl.ds(layer * rank, rank // 2, stride=2), :]
            odd = square[e, pl.ds(layer * rank + 1, rank // 2, stride=2), :]
            if layer == 0:
                odd = pltpu.roll(odd, rank, 1)
            else:
                even = pltpu.roll(even, rank, 1)
            flat = jnp.where(left, even, odd)
            for row in range(0, rank // 2, share_rows):
                share = (layer * (rank // 2) + row) // share_rows
                cut[share, e] = flat[row : row + share_rows]
    for k in range(count):
        outs[k][...] = cut[lax.bitwise_xor(me, k)]


def grads_shares(x, outer, ex_dev, seq):
    wide = x.shape[1]
    count = len(outer)
    share = (ex_dev, wide * wide // 2 // count // 128, 128)
    return pl.pallas_call(
        functools.partial(grads_kernel, count=count, seq=seq),
        out_shape=[jax.ShapeDtypeStruct(share, jnp.float32)] * count,
        in_specs=[pl.BlockSpec(memory_space=pltpu.VMEM)] * (count + 1),
        out_specs=[pl.BlockSpec(memory_space=pltpu.VMEM)] * count,
        scratch_shapes=[
            pltpu.VMEM((wide, ex_dev * seq), jnp.bfloat16),
            pltpu.VMEM((ex_dev, wide, wide), jnp.float32),
            pltpu.VMEM((count, *share), jnp.float32),
        ],
        compiler_params=pltpu.CompilerParams(vmem_limit_bytes=16 * MIB),
        cost_estimate=pl.CostEstimate(flops=10**9, bytes_accessed=4 * MIB, transcendentals=0),
    )(x, *outer)


def scores_kernel(*refs, shares, parts):
    share_refs, query_refs = refs[:shares], refs[shares : shares + parts]
    logged_ref, part_ref, flat = refs[shares + parts :]
    ex_dev, rows, lanes = share_refs[0].shape
    me = lax.axis_index("example")
    sums = [ref[...] for ref in share_refs]
    while len(sums) > 1:
        sums = [a + b for a, b in zip(sums[::2], sums[1::2])]
    flat[...] = jnp.zeros_like(flat)
    for e in range(ex_dev):
        for row in range(rows):
            flat[e : e + 1, row * lanes : (row + 1) * lanes] = sums[0][e, row : row + 1, :]
    rounded = flat[...].astype(jnp.bfloat16)
    logged_ref[...] = rounded[:ex_dev]
    width = query_refs[0].shape[0]
    for k in range(parts):
        out = lax.dot_general(rounded, query_refs[k][...], ROWS, preferred_element_type=jnp.float32)
        at = pl.multiple_of(lax.bitwise_xor(me, k) * width, width)
        part_ref[:, pl.ds(at, width)] = out[:ex_dev]


def logged_and_part(shares, queries):
    ex_dev, rows, lanes = shares[0].shape
    width = queries[0].shape[0] * len(queries)
    return pl.pallas_call(
        functools.partial(scores_kernel, shares=len(shares), parts=len(queries)),
        out_shape=[
            jax.ShapeDtypeStruct((ex_dev, rows * lanes), jnp.bfloat16),
            jax.ShapeDtypeStruct((ex_dev, width), jnp.float32),
        ],
        in_specs=[pl.BlockSpec(memory_space=pltpu.VMEM)] * (len(shares) + len(queries)),
        out_specs=[pl.BlockSpec(memory_space=pltpu.VMEM)] * 2,
        scratch_shapes=[pltpu.VMEM((16, rows * lanes), jnp.float32)],
        compiler_params=pltpu.CompilerParams(vmem_limit_bytes=24 * MIB),
        cost_estimate=pl.CostEstimate(flops=10**9, bytes_accessed=5 * MIB, transcendentals=0),
    )(*shares, *queries)


def swap(x, axis, k):
    return lax.ppermute(x, axis, [(i, i ^ k) for i in range(lax.axis_size(axis))])


def on_device(inputs, out_grads, lengths, proj_in, proj_out, queries):
    ex_dev = lengths.shape[0]
    seq = inputs.shape[1] // ex_dev
    mp = lax.axis_size("mp")
    all_queries = [queries] + [swap(queries, "example", k) for k in range(1, lax.axis_size("example"))]
    mine = project(lengths, out_grads, jnp.swapaxes(proj_out, 1, 2), seq, True, 256, 64, 3, 59)
    mine, later, all_queries[1] = lax.optimization_barrier((mine, lengths, all_queries[1]))
    outer = [mine] + [swap(mine, "mp", k) for k in range(1, mp)]
    x = project(later, inputs, jnp.swapaxes(proj_in, 1, 2), seq, False, 512, 64, 3, 32)
    shares = grads_shares(x, outer, ex_dev, seq)
    shares = [shares[0]] + [swap(shares[k], "mp", k) for k in range(1, mp)]
    logged, part = logged_and_part(shares, all_queries)
    parts = [part] + [swap(part, "mp", k) for k in range(1, mp)]
    scores = (parts[0] + parts[1]) + (parts[2] + parts[3])
    return logged, scores


def kernels_fit(inputs, out_grads, lengths, proj_in, mesh):
    shape = dict(mesh.shape)
    split = shape["groups"] * shape["example"]
    tokens, examples = inputs.shape[1] // split, lengths.shape[0] // split
    return (
        shape["mp"] == 4
        and shape["example"] == 4
        and inputs.shape[0] == 2
        and proj_in.shape[2] == 64
        and examples <= 16
        and (tokens // examples) % 256 == 0
        and (tokens // 4) % 256 == 0
    )


def solution(mesh):
    placed = (
        P(None, ("groups", "example"), "mp"),
        P(None, ("groups", "example", "mp"), None),
        P(("groups", "example")),
        P(None, "mp", None),
        P(),
        P("example", "mp"),
    )

    def whole(inputs, out_grads, lengths, proj_in, proj_out, queries):
        fit = kernels_fit(inputs, out_grads, lengths, proj_in, mesh)
        return jax.shard_map(
            on_device if fit else on_any_mesh,
            mesh=mesh,
            in_specs=placed,
            out_specs=(P(("groups", "example"), "mp"), P(("groups", "example"), None)),
            check_vma=False,
        )(inputs, out_grads, lengths, proj_in, proj_out, queries)

    return whole
```

```python
import functools

import jax
import jax.numpy as jnp
from jax import lax
from jax.experimental import pallas as pl
from jax.experimental.pallas import tpu as pltpu
from jax.sharding import PartitionSpec as P

MIB = 1 << 20
ROWS = (((1,), (1,)), ((), ()))


def outer_grads(left_rows, right_rows, ex_dev, seq_len, layers, proj_rank):
    left_wide = left_rows.astype(jnp.float32).reshape(ex_dev, seq_len, layers, proj_rank)
    right_wide = right_rows.reshape(ex_dev, seq_len, layers, proj_rank)
    return jnp.einsum("esli,eslj->elij", left_wide, right_wide, precision=lax.Precision.HIGH)


def on_any_mesh(inputs, out_grads, lengths, proj_in, proj_out, queries):
    layers = inputs.shape[0]
    tok_dev = inputs.shape[1]
    ex_dev = lengths.shape[0]
    seq_len = tok_dev // ex_dev
    proj_rank = proj_in.shape[2]
    shard_count = lax.axis_size("mp")
    tok_mp = tok_dev // shard_count
    row_base = lax.axis_index("mp") * tok_mp
    row_ids = row_base + jnp.arange(tok_mp, dtype=jnp.int32)
    owners = row_ids // seq_len
    within = row_ids % seq_len
    limits = jnp.sum(
        jnp.where(
            owners[:, None] == jnp.arange(ex_dev, dtype=jnp.int32)[None, :], lengths[None, :], 0
        ),
        axis=1,
    )
    is_live = within < limits
    projected = jnp.concatenate(
        [
            jnp.dot(out_grads[layer_idx], proj_out[layer_idx], preferred_element_type=jnp.float32)
            for layer_idx in range(layers)
        ],
        axis=1,
    )
    outer_side = jnp.where(is_live[:, None], projected, jnp.float32(0.0)).astype(jnp.bfloat16)
    outer_side = lax.optimization_barrier(outer_side)
    pieces = [
        jnp.dot(inputs[layer_idx], proj_in[layer_idx], preferred_element_type=jnp.float32)
        for layer_idx in range(layers)
    ]
    local_side = jnp.concatenate(pieces, axis=1)
    gathered = lax.all_gather(outer_side, "mp", axis=0, tiled=True)
    grads = outer_grads(gathered, local_side, ex_dev, seq_len, layers, proj_rank)
    flat_grads = grads.reshape(ex_dev, layers * proj_rank * proj_rank)
    my_share = lax.psum_scatter(flat_grads, "mp", scatter_dimension=1, tiled=True)
    logged = my_share.astype(jnp.bfloat16)
    everyone = lax.all_gather(logged, "example", axis=0, tiled=True)
    score_part = lax.dot_general(
        everyone, queries, (((1,), (1,)), ((), ())), preferred_element_type=jnp.float32
    )
    partial_scores = lax.all_to_all(score_part, "example", split_axis=0, concat_axis=1, tiled=True)
    scores = lax.psum(partial_scores, "mp")
    return (logged, scores)


def project_kernel(lens_hbm, x_hbm, w_hbm, o_ref, xbuf, wbuf, sums, lens, places, xsem, wsem, lsem, *, seq, masked):
    layers, rows, _ = x_hbm.shape
    rank = w_hbm.shape[1]
    slots, chunk, _ = xbuf.shape
    most = xsem.shape[1]
    granule = chunk // most
    half = most // 2
    base = lax.axis_index("mp") * rows if masked else 0

    lens_copy = pltpu.make_async_copy(lens_hbm, lens, lsem)
    lens_copy.start()
    weights = [
        pltpu.make_async_copy(w_hbm.at[layer], wbuf.at[pl.ds(layer * rank, rank)], wsem.at[layer])
        for layer in range(layers)
    ]
    for copy in weights:
        copy.start()
    lens_copy.wait()

    spans = []
    count = jnp.int32(0)
    for e in range(lens.shape[0]):
        low = jnp.clip(e * seq - base, 0, rows)
        high = jnp.clip(e * seq + lens[e] - base, 0, rows)
        here = lax.shift_right_logical(jnp.maximum(high - low, 0) + (granule - 1), granule.bit_length() - 1)

        def put(i, carry, low=low, at=count):
            places[at + i] = low + i * granule
            return carry

        lax.fori_loop(0, here, put, 0)
        count = count + here
        spans.append((low, high))
    total = count * layers

    def place(item):
        layer = (item >= count).astype(jnp.int32)
        return layer, pl.multiple_of(places[item - layer * count], granule)

    def in_chunk(c):
        first = jnp.maximum(c * most - half, 0)
        return first, jnp.minimum(jnp.where(c == 0, half, most), total - first)

    chunks = lax.shift_right_logical(total + half + most - 1, most.bit_length() - 1)
    chunks = jnp.where(total > 0, chunks, 0)

    def piece(item, slot, g):
        layer, row = place(item)
        return pltpu.make_async_copy(
            x_hbm.at[layer, pl.ds(row, granule)],
            xbuf.at[slot, pl.ds(g * granule, granule)],
            xsem.at[slot, g],
        )

    def each(c, slot, start):
        first, n = in_chunk(c)
        for g in range(most):

            @pl.when(g < n)
            def _():
                copy = piece(first + g, slot, g)
                copy.start() if start else copy.wait()

    for c in range(slots):

        @pl.when(c < chunks)
        def _():
            each(jnp.int32(c), c, True)

    sums[...] = jnp.zeros_like(sums)
    for copy in weights:
        copy.wait()
    second = lax.broadcasted_iota(jnp.int32, (granule, layers * rank), 1) // rank

    def compute(c, slot, parts):
        first, n = in_chunk(c)
        out = lax.dot_general(
            xbuf[slot, : parts * granule], wbuf[...], ROWS, preferred_element_type=jnp.float32
        )
        for g in range(parts):
            layer, row = place(jnp.minimum(first + g, total - 1))
            row = pl.multiple_of(jnp.where(g < n, row, rows), granule)
            at = pl.ds(row, granule)
            sums[at, :] = jnp.where(second == layer, out[g * granule : (g + 1) * granule], sums[at, :])

    def step(c, slot):
        each(c, slot, False)
        n = in_chunk(c)[1]
        pl.when(n <= half)(functools.partial(compute, c, slot, half))
        pl.when(n > half)(functools.partial(compute, c, slot, most))

        @pl.when(c + slots < chunks)
        def _():
            each(c + slots, slot, True)

        return jnp.where(slot + 1 == slots, 0, slot + 1)

    lax.fori_loop(0, chunks, step, jnp.int32(0))
    if masked:
        turned = sums[:rows].T
        token = lax.broadcasted_iota(jnp.int32, turned.shape, 1)
        live = token < 0
        for low, high in spans:
            live = live | ((token >= low) & (token < high))
        o_ref[...] = jnp.where(live, turned, 0.0).astype(o_ref.dtype)


def project(lengths, x, w, seq, masked, chunk, granule, slots, limit):
    layers, rows, depth = x.shape
    rank = w.shape[1]
    wide = layers * rank
    summed = (rows + granule, wide)
    if masked:
        out = jax.ShapeDtypeStruct((wide, rows), jnp.bfloat16)
        body = project_kernel
        more = [pltpu.VMEM(summed, jnp.float32)]
    else:
        out = jax.ShapeDtypeStruct(summed, jnp.float32)
        more = []

        def body(lens_hbm, x_hbm, w_hbm, o_ref, xbuf, wbuf, *rest, **options):
            project_kernel(lens_hbm, x_hbm, w_hbm, o_ref, xbuf, wbuf, o_ref, *rest, **options)

    return pl.pallas_call(
        functools.partial(body, seq=seq, masked=masked),
        out_shape=out,
        in_specs=[pl.BlockSpec(memory_space=pltpu.HBM)] * 3,
        out_specs=pl.BlockSpec(memory_space=pltpu.VMEM),
        scratch_shapes=[
            pltpu.VMEM((slots, chunk, depth), x.dtype),
            pltpu.VMEM((wide, depth), w.dtype),
            *more,
            pltpu.SMEM(lengths.shape, jnp.int32),
            pltpu.SMEM((rows // granule,), jnp.int32),
            pltpu.SemaphoreType.DMA((slots, chunk // granule)),
            pltpu.SemaphoreType.DMA((layers,)),
            pltpu.SemaphoreType.DMA,
        ],
        compiler_params=pltpu.CompilerParams(vmem_limit_bytes=limit * MIB),
        cost_estimate=pl.CostEstimate(
            flops=layers * rows * depth * 16, bytes_accessed=x.size // 8, transcendentals=0
        ),
    )(lengths, x, w)


def grads_kernel(x_ref, *refs, count, seq):
    outer, outs, (all_outer, square, cut) = refs[:count], refs[count : 2 * count], refs[2 * count :]
    wide, width = outer[0].shape
    examples, rank = cut.shape[1], wide // 2
    me = lax.axis_index("mp")
    for k in range(count):
        at = pl.multiple_of(lax.rem(me + count - k, count) * width, width)
        all_outer[:, pl.ds(at, width)] = outer[k][...]
    share_rows = cut.shape[2]
    left = lax.broadcasted_iota(jnp.int32, (rank // 2, wide), 1) < rank
    for e in range(examples):
        x = x_ref[e * seq : (e + 1) * seq, :]
        high = x.astype(jnp.bfloat16)
        low = (x - high.astype(jnp.float32)).astype(jnp.bfloat16)
        o = all_outer[:, e * seq : (e + 1) * seq]
        square[e] = jnp.dot(o, high, preferred_element_type=jnp.float32) + jnp.dot(
            o, low, preferred_element_type=jnp.float32
        )
        for layer in range(2):
            even = square[e, pl.ds(layer * rank, rank // 2, stride=2), :]
            odd = square[e, pl.ds(layer * rank + 1, rank // 2, stride=2), :]
            if layer == 0:
                odd = pltpu.roll(odd, rank, 1)
            else:
                even = pltpu.roll(even, rank, 1)
            flat = jnp.where(left, even, odd)
            for row in range(0, rank // 2, share_rows):
                share = (layer * (rank // 2) + row) // share_rows
                cut[share, e] = flat[row : row + share_rows]
    for k in range(count):
        outs[k][...] = cut[lax.rem(me + k, count)]


def grads_shares(x, outer, ex_dev, seq):
    wide = x.shape[1]
    count = len(outer)
    share = (ex_dev, wide * wide // 2 // count // 128, 128)
    return pl.pallas_call(
        functools.partial(grads_kernel, count=count, seq=seq),
        out_shape=[jax.ShapeDtypeStruct(share, jnp.float32)] * count,
        in_specs=[pl.BlockSpec(memory_space=pltpu.VMEM)] * (count + 1),
        out_specs=[pl.BlockSpec(memory_space=pltpu.VMEM)] * count,
        scratch_shapes=[
            pltpu.VMEM((wide, ex_dev * seq), jnp.bfloat16),
            pltpu.VMEM((ex_dev, wide, wide), jnp.float32),
            pltpu.VMEM((count, *share), jnp.float32),
        ],
        compiler_params=pltpu.CompilerParams(vmem_limit_bytes=16 * MIB),
        cost_estimate=pl.CostEstimate(flops=10**9, bytes_accessed=4 * MIB, transcendentals=0),
    )(x, *outer)


def scores_kernel(*refs, shares, parts):
    share_refs, query_refs = refs[:shares], refs[shares : shares + parts]
    logged_ref, part_ref, flat = refs[shares + parts :]
    ex_dev, rows, lanes = share_refs[0].shape
    me = lax.axis_index("example")
    sums = [ref[...] for ref in share_refs]
    while len(sums) > 1:
        sums = [a + b for a, b in zip(sums[::2], sums[1::2])]
    flat[...] = jnp.zeros_like(flat)
    for e in range(ex_dev):
        for row in range(rows):
            flat[e : e + 1, row * lanes : (row + 1) * lanes] = sums[0][e, row : row + 1, :]
    rounded = flat[...].astype(jnp.bfloat16)
    logged_ref[...] = rounded[:ex_dev]
    width = query_refs[0].shape[0]
    for k in range(parts):
        out = lax.dot_general(rounded, query_refs[k][...], ROWS, preferred_element_type=jnp.float32)
        at = pl.multiple_of(lax.bitwise_xor(me, k) * width, width)
        part_ref[:, pl.ds(at, width)] = out[:ex_dev]


def logged_and_part(shares, queries):
    ex_dev, rows, lanes = shares[0].shape
    width = queries[0].shape[0] * len(queries)
    return pl.pallas_call(
        functools.partial(scores_kernel, shares=len(shares), parts=len(queries)),
        out_shape=[
            jax.ShapeDtypeStruct((ex_dev, rows * lanes), jnp.bfloat16),
            jax.ShapeDtypeStruct((ex_dev, width), jnp.float32),
        ],
        in_specs=[pl.BlockSpec(memory_space=pltpu.VMEM)] * (len(shares) + len(queries)),
        out_specs=[pl.BlockSpec(memory_space=pltpu.VMEM)] * 2,
        scratch_shapes=[pltpu.VMEM((16, rows * lanes), jnp.float32)],
        compiler_params=pltpu.CompilerParams(vmem_limit_bytes=24 * MIB),
        cost_estimate=pl.CostEstimate(flops=10**9, bytes_accessed=5 * MIB, transcendentals=0),
    )(*shares, *queries)


def swap(x, axis, k):
    return lax.ppermute(x, axis, [(i, i ^ k) for i in range(lax.axis_size(axis))])


def turn(x, k):
    count = lax.axis_size("mp")
    return lax.ppermute(x, "mp", [(i, (i + k) % count) for i in range(count)])


def on_device(inputs, out_grads, lengths, proj_in, proj_out, queries):
    ex_dev = lengths.shape[0]
    seq = inputs.shape[1] // ex_dev
    mp = lax.axis_size("mp")
    all_queries = [queries] + [swap(queries, "example", k) for k in range(1, lax.axis_size("example"))]
    mine = project(lengths, out_grads, jnp.swapaxes(proj_out, 1, 2), seq, True, 256, 64, 3, 59)
    mine, later, all_queries[1] = lax.optimization_barrier((mine, lengths, all_queries[1]))
    outer = [mine] + [turn(mine, k) for k in range(1, mp)]
    x = project(later, inputs, jnp.swapaxes(proj_in, 1, 2), seq, False, 512, 64, 3, 32)
    shares = grads_shares(x, outer, ex_dev, seq)
    shares = [shares[0]] + [turn(shares[k], k) for k in range(1, mp)]
    logged, part = logged_and_part(shares, all_queries)
    parts = [part] + [swap(part, "mp", k) for k in range(1, mp)]
    scores = (parts[0] + parts[1]) + (parts[2] + parts[3])
    return logged, scores


def kernels_fit(inputs, out_grads, lengths, proj_in, mesh):
    shape = dict(mesh.shape)
    split = shape["groups"] * shape["example"]
    tokens, examples = inputs.shape[1] // split, lengths.shape[0] // split
    return (
        shape["mp"] == 4
        and shape["example"] == 4
        and inputs.shape[0] == 2
        and proj_in.shape[2] == 64
        and examples <= 16
        and (tokens // examples) % 256 == 0
        and (tokens // 4) % 256 == 0
    )


def solution(mesh):
    placed = (
        P(None, ("groups", "example"), "mp"),
        P(None, ("groups", "example", "mp"), None),
        P(("groups", "example")),
        P(None, "mp", None),
        P(),
        P("example", "mp"),
    )

    def whole(inputs, out_grads, lengths, proj_in, proj_out, queries):
        fit = kernels_fit(inputs, out_grads, lengths, proj_in, mesh)
        return jax.shard_map(
            on_device if fit else on_any_mesh,
            mesh=mesh,
            in_specs=placed,
            out_specs=(P(("groups", "example"), "mp"), P(("groups", "example"), None)),
            check_vma=False,
        )(inputs, out_grads, lengths, proj_in, proj_out, queries)

    return whole
```
